32 devices in a mesh: dp: 4 (over z), expert: 8 (over y, x, core).
Axes of the slice: x: 2, y: 2, z: 4, core: 2. Of those that a mesh axis runs over, the one named last changes fastest.
Arguments:
- queries: bfloat16 [4352, 1536], P(('dp', 'expert')), may hold values from -6 to 6
- fresh_keys: bfloat16 [4352, 256], P(('dp', 'expert')), may hold values from -1 to 1
- fresh_values: bfloat16 [4352, 256], P(('dp', 'expert')), may hold values from -6 to 6
- residual: bfloat16 [4352, 1536], P(('dp', 'expert')), may hold values from -6 to 6
- norm_gain: float32 [1536], replicated, may hold values from 0.25 to 1.75
- out_weight: bfloat16 [1536, 1536], replicated, may hold values from -0.15625 to 0.15625
- router_weight: bfloat16 [1536, 8], replicated, may hold values from -0.15625 to 0.15625
- gate_weight: bfloat16 [8, 1536, 384], P('expert'), may hold values from -0.15625 to 0.15625
- up_weight: bfloat16 [8, 1536, 384], P('expert'), may hold values from -0.15625 to 0.15625
- down_weight: bfloat16 [8, 384, 1536], P('expert'), may hold values from -0.3125 to 0.3125
- expert_ids: int32 [4352, 4], P(('dp', 'expert')), may hold values from 0 to 7, all different within a row; in each aligned block of 136 rows (0 to 135, 136 to 271, ...) at most 104 rows name the same one
- paged_keys: bfloat16 [384, 128, 256], P(('dp', 'expert')), may hold values from -1 to 1
- paged_values: bfloat16 [384, 128, 256], P(('dp', 'expert')), may hold values from -6 to 6
- decode_table: int32 [224, 4], P(('dp', 'expert')), may hold values from 0 to 11
- prefill_table: int32 [32, 4], P(('dp', 'expert')), may hold values from 0 to 11
- decode_len: int32 [32, 8], P(('dp', 'expert')), may hold values from 1 to 511, 2048 in all within a row
- prefill_len: int32 [32], P(('dp', 'expert')), may hold values from 0 to 512
- departing_keys: bfloat16 [32, 512, 256], P(('dp', 'expert')), may hold values from -1 to 1
- departing_values: bfloat16 [32, 512, 256], P(('dp', 'expert')), may hold values from -6 to 6
- destination: int32 [8, 4], P('expert'), may hold values from 0 to 3, each once within a row
Outputs:
- layer_out: bfloat16 [4352, 1536], P(('dp', 'expert'))
- moved_keys: bfloat16 [32, 512, 256], P(('dp', 'expert'))
- moved_values: bfloat16 [32, 512, 256], P(('dp', 'expert'))
The draws below stay inside these ranges and needn't reach their ends.
Inputs may be any that keep to these rules, and one draw needn't show every extreme that they name: `expert_ids`: in each device's 136 rows no expert is named by more than 104 rows, a bound that some block reaches. `decode_len`: each device's 8 lengths sum to 2048 and the largest is 511. `destination`: each row is a permutation of the dp indices. `decode_table`: entries index pages of the device's own pool. `prefill_table`: entries index pages of the device's own pool.
All inputs are finite; a program needn't handle non-finite values.
Results may differ from the reference program's by a relative error of at most 0.0045.
Values may be sent and summed in bfloat16 or wider, within the bound.
A program may use at most 128 MiB of HBM per device.

```python
import math
import jax
import jax.numpy as jnp
import numpy as np
from jax import lax

D = 1536
QUERY_HEADS = 12
KEY_VALUE_HEADS = 2
HEAD_SIZE = 128
FF = 384
TOPK = 4
PAGE_TOKENS = 128
MAXP = 4
POOL_PAGES = 12
DEC_DEV = 8
PCH = 128
E = 8
CONTEXT_LENGTH = 512
DEVICE_TOKENS = 136
CAP = 104
N_DP = 4
N_EXPERT = 8
DEVICES = 32


def plant(values, key, low, high):
    index_at = [jax.random.randint(jax.random.fold_in(key, axis), (), 0, length) for axis, length in enumerate(values.shape)]
    main_axis = values.shape.index(max(values.shape))
    beside = index_at[:main_axis] + [(index_at[main_axis] + 1) % values.shape[main_axis]] + index_at[main_axis + 1:]
    return values.at[tuple(index_at)].set(low).at[tuple(beside)].set(high)


def block_scale(rng, extent, cuts, smallest, high):
    gain = 1.0
    for axis_at, shards_of in cuts:
        draws = jax.random.uniform(jax.random.fold_in(jax.random.fold_in(rng, 6), axis_at), (shards_of,), jnp.float32, smallest / len(cuts), high / len(cuts))
        gain = gain * jnp.repeat(jnp.exp(draws), extent[axis_at] // shards_of).reshape((-1,) + (1,) * (len(extent) - 1 - axis_at))
    return gain


def length_profile(count, total, limit, skew):
    loads = [(1 << 20) // math.isqrt(standing ** skew) + 1 for standing in range(2, count + 1)]
    spare, counts = total - limit - (count - 1), [1] * (count - 1)
    while spare > 0:
        movable = [i for i in range(count - 1) if counts[i] < limit]
        pool, remaining = sum([loads[i] for i in movable]), spare
        for i in movable:
            addition = min(limit - counts[i], max(1, remaining * loads[i] // pool), spare)
            counts[i] = counts[i] + addition
            spare = spare - addition
    return np.array([limit] + counts)


def uneven_parts(own_key, count, total, limit, lean):
    if count == 2:
        one = jax.random.randint(own_key, (), max(1, total - limit), min(limit, total - 1) + 1)
        return jnp.stack([one, total - one])
    tallies = jnp.asarray(length_profile(count, total, limit, lean), jnp.int32)
    twos = (count - 1) // 2
    giver, receiver = tallies[1:1 + 2 * twos:2], tallies[2:2 + 2 * twos:2]
    room = jnp.minimum(giver - 1, limit - receiver)
    moved = jax.random.randint(jax.random.fold_in(own_key, 1), (twos,), 0, 1 << 20) % (room + 1)
    tallies = tallies.at[1:1 + 2 * twos:2].set(giver - moved).at[2:2 + 2 * twos:2].set(receiver + moved)
    return tallies[jax.random.permutation(jax.random.fold_in(own_key, 2), count)]


def deal_out(rng, own, number, rows, amount, top, bound, skew):
    order = jax.random.permutation(rng, amount)
    heavy_load, common = shares(amount, rows * top, bound, skew, True), shares(amount, rows * top, bound, skew, False)
    places = jnp.arange(amount)

    def named(sizes, offset_by):
        used = int((sizes > 0).sum())
        fixed = max(1, used // 4)
        passed = fixed + (places - fixed + offset_by * (used - fixed)) % max(1, amount - fixed)
        return jnp.zeros((amount,), jnp.int32).at[order[jnp.where(places < fixed, places, passed)]].set(jnp.asarray(sizes, jnp.int32))

    sizes = jnp.where(number % 4 == 0, named(heavy_load, number // 4), named(common, number - number // 4 - 1))
    mixed = jax.random.permutation(jax.random.fold_in(own, 3), amount)
    donor, sink = mixed[0:amount // 2 * 2:2], mixed[1:amount // 2 * 2:2]
    slack = jnp.minimum(sizes[donor] - 1, bound - sizes[sink]) // 2
    slack = jnp.where((donor == order[0]) | (sink == order[0]) | (sizes[sink] == 0), 0, jnp.maximum(slack, 0))
    passed = jax.random.randint(jax.random.fold_in(own, 4), (amount // 2,), 0, 1 << 20) % (slack + 1)
    sizes = sizes.at[donor].add(-passed).at[sink].add(passed)
    labels = jnp.searchsorted(jnp.cumsum(sizes), jnp.arange(rows * top), side="right").astype(jnp.int32)
    table = labels.reshape(top, rows).T
    table = table[jax.random.permutation(jax.random.fold_in(own, 1), rows)]
    offset_by = jax.random.randint(jax.random.fold_in(own, 2), (rows, 1), 0, top)
    return jnp.take_along_axis(table, (jnp.arange(top)[None, :] + offset_by) % top, axis=1)


def shares(amount, total, bound, skew, full):
    weights = [(1 << 20) // math.isqrt(grade ** skew) + 1 for grade in range(1, amount + 1)]
    largest = bound if full else min(bound, max(-(-total // amount), total * weights[0] // sum(weights)))
    least = 1 if total - largest >= amount - 1 else 0
    holding, surplus = [largest] + [least] * (amount - 1), total - largest - least * (amount - 1)
    while surplus > 0:
        candidates = [i for i in range(1, amount) if holding[i] < largest] or [i for i in range(1, amount) if holding[i] < bound]
        mass, budget = sum([weights[i] for i in candidates]), surplus
        for i in candidates:
            more = min(bound - holding[i], max(1, budget * weights[i] // mass), surplus)
            holding[i] = holding[i] + more
            surplus = surplus - more
    return np.array(holding)


def noise(rng, extent, deviation, reach, pieces=(), held_as=jnp.bfloat16):
    drawn = deviation * jax.random.normal(rng, extent, jnp.float32)
    if pieces:
        drawn = drawn * block_scale(rng, extent, pieces, -0.22, 0.18)
    return jnp.clip(drawn, -reach, reach).astype(held_as)


def setup_inputs(seed: int = 0) -> dict:
    streams_of = jax.random.split(jax.random.key(seed), 21)
    queries = noise(streams_of[0], (DEVICES * DEVICE_TOKENS, QUERY_HEADS * HEAD_SIZE), 1.0, 6.0, ((0, 32),))
    fresh_keys = jnp.clip(jax.random.uniform(streams_of[1], (DEVICES * DEVICE_TOKENS, KEY_VALUE_HEADS * HEAD_SIZE), jnp.float32, -1.0, 1.0) * block_scale(streams_of[1], (DEVICES * DEVICE_TOKENS, KEY_VALUE_HEADS * HEAD_SIZE), ((0, 32),), -0.4, 0.0), -1.0, 1.0).astype(jnp.bfloat16)
    fresh_values = noise(streams_of[2], (DEVICES * DEVICE_TOKENS, KEY_VALUE_HEADS * HEAD_SIZE), 1.0, 6.0, ((0, 32),))
    residual = noise(streams_of[3], (DEVICES * DEVICE_TOKENS, D), 1.0, 6.0, ((0, 32),))
    norm_gain = jnp.clip(1.0 + 0.15 * jax.random.normal(streams_of[4], (D,), jnp.float32), 0.25, 1.75)
    out_weight = noise(streams_of[5], (QUERY_HEADS * HEAD_SIZE, D), (QUERY_HEADS * HEAD_SIZE) ** -0.5, 0.15625)
    router_weight = noise(streams_of[6], (D, E), D ** -0.5, 0.15625)
    gate_weight = noise(streams_of[7], (E, D, FF), D ** -0.5, 0.15625, ((0, 8),))
    up_weight = noise(streams_of[8], (E, D, FF), D ** -0.5, 0.15625, ((0, 8),))
    down_weight = noise(streams_of[9], (E, FF, D), FF ** -0.5, 0.3125, ((0, 8),))
    expert_ids_keys = jax.random.split(jax.random.fold_in(streams_of[10], 1), (DEVICES * DEVICE_TOKENS) // DEVICE_TOKENS)
    expert_ids_turns = jax.random.permutation(jax.random.fold_in(streams_of[10], 3), (DEVICES * DEVICE_TOKENS) // DEVICE_TOKENS)
    expert_ids = jax.vmap(lambda own, number: deal_out(jax.random.fold_in(streams_of[10], 2), own, number, DEVICE_TOKENS, E, TOPK, CAP, 2))(expert_ids_keys, expert_ids_turns).reshape((DEVICES * DEVICE_TOKENS, TOPK))
    paged_keys = jnp.clip(jax.random.uniform(streams_of[11], (DEVICES * POOL_PAGES, PAGE_TOKENS, KEY_VALUE_HEADS * HEAD_SIZE), jnp.float32, -1.0, 1.0) * block_scale(streams_of[11], (DEVICES * POOL_PAGES, PAGE_TOKENS, KEY_VALUE_HEADS * HEAD_SIZE), ((0, 32),), -0.4, 0.0), -1.0, 1.0).astype(jnp.bfloat16)
    paged_values = noise(streams_of[12], (DEVICES * POOL_PAGES, PAGE_TOKENS, KEY_VALUE_HEADS * HEAD_SIZE), 1.0, 6.0, ((0, 32),))
    decode_table = plant(jax.random.randint(streams_of[13], (DEVICES * (DEC_DEV - 1), MAXP), 0, POOL_PAGES), jax.random.fold_in(streams_of[13], 1), 0, POOL_PAGES - 1).astype(jnp.int32)
    prefill_table = plant(jax.random.randint(streams_of[14], (DEVICES, MAXP), 0, POOL_PAGES), jax.random.fold_in(streams_of[14], 1), 0, POOL_PAGES - 1).astype(jnp.int32)
    decode_len = jax.vmap(lambda own: uneven_parts(own, DEC_DEV, DEC_DEV * CONTEXT_LENGTH // 2, CONTEXT_LENGTH - 1, 2))(jax.random.split(streams_of[15], DEVICES)).reshape((DEVICES, DEC_DEV)).astype(jnp.int32)
    prefill_len = plant(jax.random.randint(streams_of[16], (DEVICES,), 0, CONTEXT_LENGTH + 1), jax.random.fold_in(streams_of[16], 1), 0, CONTEXT_LENGTH).astype(jnp.int32)
    departing_keys = jnp.clip(jax.random.uniform(streams_of[17], (DEVICES, CONTEXT_LENGTH, KEY_VALUE_HEADS * HEAD_SIZE), jnp.float32, -1.0, 1.0) * block_scale(streams_of[17], (DEVICES, CONTEXT_LENGTH, KEY_VALUE_HEADS * HEAD_SIZE), ((0, 32),), -0.4, 0.0), -1.0, 1.0).astype(jnp.bfloat16)
    departing_values = noise(streams_of[18], (DEVICES, CONTEXT_LENGTH, KEY_VALUE_HEADS * HEAD_SIZE), 1.0, 6.0, ((0, 32),))
    destination = jax.vmap(lambda own: jax.random.permutation(own, N_DP))(jax.random.split(streams_of[19], N_EXPERT)).reshape((N_EXPERT, N_DP)).astype(jnp.int32)
    return dict(queries=queries, fresh_keys=fresh_keys, fresh_values=fresh_values, residual=residual, norm_gain=norm_gain, out_weight=out_weight, router_weight=router_weight, gate_weight=gate_weight, up_weight=up_weight, down_weight=down_weight, expert_ids=expert_ids, paged_keys=paged_keys, paged_values=paged_values, decode_table=decode_table, prefill_table=prefill_table, decode_len=decode_len, prefill_len=prefill_len, departing_keys=departing_keys, departing_values=departing_values, destination=destination)


def attend(query_row_block, key_row_block, value_row_block, valid):
    batch_groups = query_row_block.shape[0]
    query_total = query_row_block.shape[1]
    key_total = key_row_block.shape[1]
    grouped_rows = query_row_block.reshape(batch_groups, query_total, KEY_VALUE_HEADS, QUERY_HEADS // KEY_VALUE_HEADS, HEAD_SIZE).astype(jnp.float32)
    key_head_rows = key_row_block.reshape(batch_groups, key_total, KEY_VALUE_HEADS, HEAD_SIZE).astype(jnp.float32)
    value_head_rows = value_row_block.reshape(batch_groups, key_total, KEY_VALUE_HEADS, HEAD_SIZE).astype(jnp.float32)
    scores = jnp.einsum('bqhgd,bkhd->bqhgk', grouped_rows, key_head_rows) * HEAD_SIZE ** (-0.5)
    weights = jnp.where(valid[:, :, None, None, :], jnp.exp(scores), 0.0)
    totals = lax.optimization_barrier(jnp.sum(weights, axis=-1))
    rounded = lax.optimization_barrier(weights.astype(jnp.bfloat16)).astype(jnp.float32)
    mixed = jnp.einsum('bqhgk,bkhd->bqhgd', rounded, value_head_rows) / totals[..., None]
    return mixed.reshape(batch_groups, query_total, QUERY_HEADS * HEAD_SIZE).astype(jnp.bfloat16)

def device_attention(operands):
    queries, fresh_keys, fresh_values, paged_keys, paged_values, decode_table, prefill_table, decode_len, prefill_len, arrived_keys, arrived_values = operands
    width_total = KEY_VALUE_HEADS * HEAD_SIZE
    resident_keys = paged_keys[decode_table].reshape(DEC_DEV - 1, CONTEXT_LENGTH, width_total)
    resident_values = paged_values[decode_table].reshape(DEC_DEV - 1, CONTEXT_LENGTH, width_total)
    cache_keys = jnp.concatenate([resident_keys, arrived_keys[None]], axis=0)
    cache_values = jnp.concatenate([resident_values, arrived_values[None]], axis=0)
    decode_keys = jnp.concatenate([cache_keys, fresh_keys[:DEC_DEV, None]], axis=1)
    decode_values = jnp.concatenate([cache_values, fresh_values[:DEC_DEV, None]], axis=1)
    positions = jnp.arange(CONTEXT_LENGTH, dtype=jnp.int32)
    decode_valid = jnp.concatenate([positions[None, :] < decode_len[:, None], jnp.ones((DEC_DEV, 1), dtype=bool)], axis=1)[:, None, :]
    decode_out = attend(queries[:DEC_DEV, None], decode_keys, decode_values, decode_valid)[:, 0]
    context_keys = paged_keys[prefill_table].reshape(CONTEXT_LENGTH, width_total)
    context_values = paged_values[prefill_table].reshape(CONTEXT_LENGTH, width_total)
    block_keys = jnp.concatenate([context_keys, fresh_keys[DEC_DEV:]], axis=0)[None]
    block_values = jnp.concatenate([context_values, fresh_values[DEC_DEV:]], axis=0)[None]
    block_pos = jnp.arange(PCH, dtype=jnp.int32)
    context_valid = jnp.broadcast_to(positions[None, :] < prefill_len, (PCH, CONTEXT_LENGTH))
    causal = block_pos[None, :] <= block_pos[:, None]
    block_valid = jnp.concatenate([context_valid, causal], axis=1)[None]
    block_out = attend(queries[DEC_DEV:][None], block_keys, block_values, block_valid)[0]
    return jnp.concatenate([decode_out, block_out], axis=0)

def reference(queries, fresh_keys, fresh_values, residual, norm_gain, out_weight, router_weight, gate_weight, up_weight, down_weight, expert_ids, paged_keys, paged_values, decode_table, prefill_table, decode_len, prefill_len, departing_keys, departing_values, destination):
    device_count = N_DP * N_EXPERT
    width_total = KEY_VALUE_HEADS * HEAD_SIZE
    device_ids = jnp.arange(device_count, dtype=jnp.int32)
    column = device_ids % N_EXPERT
    targets = destination[column, device_ids // N_EXPERT] * N_EXPERT + column
    arrived_keys = jnp.zeros_like(departing_keys).at[targets].set(departing_keys)
    arrived_values = jnp.zeros_like(departing_values).at[targets].set(departing_values)
    operands = (queries.reshape(device_count, DEVICE_TOKENS, QUERY_HEADS * HEAD_SIZE), fresh_keys.reshape(device_count, DEVICE_TOKENS, width_total), fresh_values.reshape(device_count, DEVICE_TOKENS, width_total), paged_keys.reshape(device_count, POOL_PAGES, PAGE_TOKENS, width_total), paged_values.reshape(device_count, POOL_PAGES, PAGE_TOKENS, width_total), decode_table.reshape(device_count, DEC_DEV - 1, MAXP), prefill_table, decode_len, prefill_len, arrived_keys, arrived_values)
    attended = lax.map(device_attention, operands).reshape(device_count * DEVICE_TOKENS, QUERY_HEADS * HEAD_SIZE)
    hidden = residual.astype(jnp.float32) + jnp.dot(attended, out_weight, preferred_element_type=jnp.float32)
    variance = lax.optimization_barrier(jnp.mean(hidden * hidden, axis=-1, keepdims=True))
    normed = (hidden * lax.rsqrt(variance + 1e-06) * norm_gain).astype(jnp.bfloat16)
    logits = jnp.dot(normed, router_weight, preferred_element_type=jnp.float32)
    chosen = jax.nn.sigmoid(jnp.take_along_axis(logits, expert_ids, axis=1))
    gates = chosen / lax.optimization_barrier(jnp.sum(chosen, axis=1, keepdims=True))
    flat_ids = expert_ids.reshape(-1)
    flat_gates = gates.reshape(-1)
    slots = device_count * CAP

    def expert_step(accum, operand):
        gate_mat, up_mat, down_mat, expert_index = operand
        hits = flat_ids == expert_index
        route_rows = jnp.nonzero(hits, size=slots, fill_value=0)[0]
        live = jnp.arange(slots) < jnp.sum(hits.astype(jnp.int32))
        token_rows = route_rows // TOPK
        gathered = normed[token_rows]
        gate_part = jnp.dot(gathered, gate_mat, preferred_element_type=jnp.float32)
        up_part = jnp.dot(gathered, up_mat, preferred_element_type=jnp.float32)
        inner = (jax.nn.relu(gate_part) * up_part).astype(jnp.bfloat16)
        expert_out = jnp.dot(inner, down_mat, preferred_element_type=jnp.float32).astype(jnp.bfloat16)
        factor = jnp.where(live, flat_gates[route_rows], 0.0)
        accum = accum.at[token_rows].add(factor[:, None] * expert_out.astype(jnp.float32))
        return (accum, None)
    mixture, _ = lax.scan(expert_step, jnp.zeros(hidden.shape, jnp.float32), (gate_weight, up_weight, down_weight, jnp.arange(E, dtype=jnp.int32)))
    layer_out = (hidden + mixture).astype(jnp.bfloat16)
    new_rows = DEC_DEV - 1 + jnp.arange(device_count, dtype=jnp.int32) * DEVICE_TOKENS
    last_keys = fresh_keys[new_rows]
    last_values = fresh_values[new_rows]
    last_len = decode_len[:, DEC_DEV - 1]

    def write_row(cache, row, where_at):
        return lax.dynamic_update_slice(cache, row[None], (where_at, jnp.zeros((), jnp.int32)))
    moved_keys = jax.vmap(write_row)(arrived_keys, last_keys, last_len)
    moved_values = jax.vmap(write_row)(arrived_values, last_values, last_len)
    return (layer_out, moved_keys, moved_values)
```

```python
import functools

import jax
import jax.numpy as jnp
from jax import lax
from jax.experimental import pallas as pl
from jax.experimental.pallas import tpu as pltpu
from jax.sharding import PartitionSpec as P

QUERY_HEADS = 12
KEY_VALUE_HEADS = 2
GROUP = QUERY_HEADS // KEY_VALUE_HEADS
HEAD = 128
DEC = 8
SCALE = HEAD ** (-0.5)
MESH = pl.DeviceIdType.MESH
F32 = jnp.float32
BF16 = jnp.bfloat16
NT = (((1,), (1,)), ((), ()))


def iota(shape, dim):
    return lax.broadcasted_iota(jnp.int32, shape, dim)


def kernel(
    n_dp, n_ex,
    dec_table, pre_table, dec_len, pre_len, destination,
    queries, fresh_k, fresh_v, residual, gain, router, ids, pool_k, pool_v, dep_k, dep_v,
    out_w, gate_w, up_w, down_w,
    layer_out, moved_k, moved_v,
    wo, wg, wu, wd, hidden, attended, masks, tokens, partial, inbox,
    ask, answer, asked, answered, got_k, got_v,
    w_sem, ask_s, ask_r, ans_s, ans_r, mk_s, mk_r, mv_s, mv_r, msk_s, msk_r, g_s, g_r, r_s, r_r,
):
    row = lax.axis_index("dp")
    me = lax.axis_index("expert")
    count = queries.shape[0]
    padded = tokens.shape[1]
    cut = (padded // 2 + 15) // 16 * 16
    spans = ((0, cut), (cut, padded - cut))
    pool_pages, page = pool_k.shape[0], pool_k.shape[1]
    context = dep_k.shape[1]
    steps = n_ex.bit_length() - 1
    bits = [1 << b for b in range(steps)]
    orders = (bits[1:] + bits[:1], bits[1:][::-1] + bits[:1])

    weights = [
        pltpu.make_async_copy(src, dst, w_sem.at[i])
        for i, (src, dst) in enumerate(((out_w, wo), (gate_w.at[0], wg), (up_w.at[0], wu), (down_w.at[0], wd)))
    ]
    for copy in weights:
        copy.start()

    barrier = pltpu.get_barrier_semaphore()
    for d in range(1, n_dp):
        pl.semaphore_signal(barrier, inc=1, device_id={"dp": (row + d) % n_dp}, device_id_type=MESH)
    for d in range(1, n_ex):
        pl.semaphore_signal(barrier, inc=1, device_id={"expert": (me + d) % n_ex}, device_id_type=MESH)
    pl.semaphore_wait(barrier, n_dp + n_ex - 2)

    last = queries[0:16, :].astype(F32)[DEC - 1:DEC, :]
    line = iota((16, HEAD), 0)
    message = jnp.zeros((16, HEAD), F32)
    for h in range(QUERY_HEADS):
        message = jnp.where(line == h, last[:, h * HEAD:(h + 1) * HEAD], message)
    last_len = dec_len[0, DEC - 1]
    message = jnp.where(line == QUERY_HEADS, (last_len // 16).astype(F32), message)
    message = jnp.where(line == QUERY_HEADS + 1, (last_len % 16).astype(F32), message)
    ask[...] = message.astype(BF16)
    asked[row] = message.astype(BF16)

    def to_row(src, dst, send, recv, d):
        return pltpu.make_async_remote_copy(
            src_ref=src, dst_ref=dst.at[row], send_sem=send.at[d], recv_sem=recv.at[d],
            device_id={"dp": (row + d) % n_dp}, device_id_type=MESH)

    def from_row(src, dst, send, recv, d):
        return pltpu.make_async_remote_copy(
            src_ref=src, dst_ref=dst.at[(row + n_dp - d) % n_dp], send_sem=send.at[d], recv_sem=recv.at[d],
            device_id={"dp": (row + d) % n_dp}, device_id_type=MESH)

    for d in range(1, n_dp):
        to_row(ask, asked, ask_s, ask_r, d).start()

    chose = jnp.zeros((count, HEAD), F32)
    lane = iota((count, HEAD), 1)
    for k in range(ids.shape[1]):
        chose = jnp.where(ids[:, k:k + 1] == lane, 1.0, chose)
    masks[me] = jnp.concatenate([chose, jnp.zeros((padded - count, HEAD), F32)], axis=0).astype(BF16)

    def mask_copy(d, slot):
        return pltpu.make_async_remote_copy(
            src_ref=masks.at[slot], dst_ref=masks.at[slot], send_sem=msk_s.at[d], recv_sem=msk_r.at[d],
            device_id={"expert": (me + d) % n_ex}, device_id_type=MESH)

    for d in range(1, n_ex):
        mask_copy(d, me).start()

    for d in range(1, n_dp):
        to_row(dep_k.at[0], got_k, mk_s, mk_r, d).start()
        to_row(dep_v.at[0], got_v, mv_s, mv_r, d).start()
    got_k[row] = dep_k[0]
    got_v[row] = dep_v[0]

    small = iota((16, page), 0)
    spot = iota((16, page), 1)
    lens = jnp.zeros((16, page), jnp.int32)
    tables = [jnp.full((16, page), -1, jnp.int32) for _ in range(dec_table.shape[1])]
    for s in range(DEC - 1):
        lens = jnp.where(small == s, dec_len[0, s], lens)
        for p in range(len(tables)):
            tables[p] = jnp.where(small == s, dec_table[s, p], tables[p])
    pieces = []
    for g in range(pool_pages):
        piece = jnp.zeros((16, page), F32)
        for p, table in enumerate(tables):
            piece += jnp.where((table == g) & (spot + p * page < lens), 1.0, 0.0)
        pieces.append(piece)
    times = jnp.concatenate(pieces, axis=1)
    times = jnp.concatenate([times] * GROUP, axis=0)

    def decode_part(kh):
        cols = slice(kh * HEAD, (kh + 1) * HEAD)
        q = jnp.concatenate(
            [queries[0:16, (kh * GROUP + g) * HEAD:(kh * GROUP + g + 1) * HEAD] for g in range(GROUP)], axis=0)
        keys = pool_k[:, :, cols].reshape(pool_pages * page, HEAD)
        values = pool_v[:, :, cols].reshape(pool_pages * page, HEAD)
        s = lax.dot_general(q, keys, NT, preferred_element_type=F32) * SCALE
        w = jnp.exp(s) * times
        return jnp.dot(w.astype(BF16), values, preferred_element_type=F32), jnp.sum(w, axis=1, keepdims=True)

    decoded = [decode_part(kh) for kh in range(KEY_VALUE_HEADS)]

    for d in range(1, n_dp):
        from_row(ask, asked, ask_s, ask_r, d).wait_recv()
    q = asked[...].reshape(n_dp * 16, HEAD)
    meta = asked[...].astype(F32)
    limits = meta[:, QUERY_HEADS:QUERY_HEADS + 1, 0:1] * 16.0 + meta[:, QUERY_HEADS + 1:QUERY_HEADS + 2, 0:1]
    limits = jnp.broadcast_to(limits, (n_dp, 16, 1)).reshape(n_dp * 16, 1)
    live = iota((n_dp * 16, context), 1).astype(F32) < limits
    head_line = iota((n_dp * 16, 1), 0) % 16
    sums, totals = None, None
    for kh in range(KEY_VALUE_HEADS):
        cols = slice(kh * HEAD, (kh + 1) * HEAD)
        s = lax.dot_general(q, dep_k[0, :, cols], NT, preferred_element_type=F32) * SCALE
        mine = (head_line >= kh * GROUP) & (head_line < (kh + 1) * GROUP)
        w = jnp.where(live & mine, jnp.exp(s), 0.0)
        mixed = jnp.dot(w.astype(BF16), dep_v[0, :, cols], preferred_element_type=F32)
        total = jnp.sum(w, axis=1, keepdims=True)
        sums = mixed if sums is None else sums + mixed
        totals = total if totals is None else totals + total
    answer[:, 0:16, :] = sums.reshape(n_dp, 16, HEAD)
    answer[:, 16:32, :] = jnp.broadcast_to(totals, (n_dp * 16, HEAD)).reshape(n_dp, 16, HEAD)
    answered[row] = answer[row]

    def reply(d, slot):
        return pltpu.make_async_remote_copy(
            src_ref=answer.at[(row + d) % n_dp], dst_ref=answered.at[slot],
            send_sem=ans_s.at[d], recv_sem=ans_r.at[d],
            device_id={"dp": (row + d) % n_dp}, device_id_type=MESH)

    for d in range(1, n_dp):
        reply(d, row).start()

    r = iota((count, context), 0)
    c = iota((count, context), 1)
    context_valid = (r >= DEC) & (c < pre_len[0])
    r = iota((count, count), 0)
    c = iota((count, count), 1)
    fresh_valid = (c <= r) & ((c >= DEC) | (c == r))
    fresh_parts = []
    for kh in range(KEY_VALUE_HEADS):
        cols = slice(kh * HEAD, (kh + 1) * HEAD)
        picks = [pre_table[0, p] for p in range(pre_table.shape[1])]
        keys = jnp.concatenate([pool_k[p, :, cols] for p in picks], axis=0)
        values = jnp.concatenate([pool_v[p, :, cols] for p in picks], axis=0)
        for g in range(GROUP):
            h = kh * GROUP + g
            q = queries[:, h * HEAD:(h + 1) * HEAD]
            s = lax.dot_general(q, keys, NT, preferred_element_type=F32) * SCALE
            w = jnp.where(context_valid, jnp.exp(s), 0.0)
            s = lax.dot_general(q, fresh_k[:, cols], NT, preferred_element_type=F32) * SCALE
            wf = jnp.where(fresh_valid, jnp.exp(s), 0.0)
            total = jnp.sum(w, axis=1, keepdims=True) + jnp.sum(wf, axis=1, keepdims=True)
            mixed = jnp.dot(w.astype(BF16), values, preferred_element_type=F32)
            mixed += jnp.dot(wf.astype(BF16), fresh_v[:, cols], preferred_element_type=F32)
            part, part_total = decoded[kh]
            fresh_parts.append((
                mixed[0:DEC] + part[g * 16:g * 16 + DEC],
                total[0:DEC] + part_total[g * 16:g * 16 + DEC],
            ))
            attended[DEC:count, h * HEAD:(h + 1) * HEAD] = mixed[DEC:] / total[DEC:]

    for d in range(1, n_dp):
        reply(d, (row + n_dp - d) % n_dp).wait_recv()
    arrived = jnp.zeros((32, HEAD), F32)
    for i in range(n_dp):
        arrived = jnp.where(destination[0, i] == row, answered[i], arrived)
    seventh = iota((DEC, HEAD), 0) == DEC - 1
    for h in range(QUERY_HEADS):
        mixed, total = fresh_parts[h]
        mixed = mixed + jnp.where(seventh, arrived[h:h + 1, :], 0.0)
        total = total + jnp.where(seventh, arrived[16 + h:17 + h, :], 0.0)
        attended[0:DEC, h * HEAD:(h + 1) * HEAD] = mixed / total

    weights[0].wait()
    x = residual[...].astype(F32) + jnp.dot(attended[...].astype(BF16), wo[...], preferred_element_type=F32)
    hidden[...] = x
    variance = jnp.mean(x * x, axis=-1, keepdims=True)
    normed = x * lax.rsqrt(variance + 1e-06) * gain[...]
    tokens[me] = jnp.concatenate([normed, jnp.zeros((padded - count, x.shape[1]), F32)], axis=0).astype(BF16)

    def flip(index, flips):
        for b in flips:
            index = index + b - 2 * b * ((index // b) % 2)
        return index

    def place(half, flips):
        return sum(1 << orders[half].index(b) for b in flips)

    def flips_of(half, subset):
        return [orders[half][k] for k in range(steps) if subset >> k & 1]

    def gather_copy(half, subset, k, arriving):
        start, size = spans[half]
        owner = flip(me, flips_of(half, subset + (1 << k) if arriving else subset))
        block = tokens.at[owner, pl.ds(start, size)]
        sem = half * n_ex + (1 << k) + subset
        return pltpu.make_async_remote_copy(
            src_ref=block, dst_ref=block, send_sem=g_s.at[sem], recv_sem=g_r.at[sem],
            device_id={"expert": flip(me, [orders[half][k]])}, device_id_type=MESH)

    def forward(half, subset):
        for k in range(subset.bit_length(), steps):
            gather_copy(half, subset, k, False).start()

    def take(half, subset):
        k = subset.bit_length() - 1
        gather_copy(half, subset - (1 << k), k, True).wait_recv()

    for half in range(2):
        forward(half, 0)
    for d in range(1, n_ex):
        mask_copy(d, (me + n_ex - d) % n_ex).wait_recv()
    for copy in weights[1:]:
        copy.wait()

    def expert(owner):
        x = tokens[owner]
        logits = jnp.dot(x, router[...], preferred_element_type=F32)
        score = jax.nn.sigmoid(logits) * masks[owner].astype(F32)[:, 0:n_ex]
        total = jnp.sum(score, axis=1, keepdims=True)
        mine = jnp.sum(jnp.where(iota((padded, n_ex), 1) == me, score, 0.0), axis=1, keepdims=True)
        gate = mine / jnp.where(total == 0.0, 1.0, total)
        inner = jnp.maximum(jnp.dot(x, wg[...], preferred_element_type=F32), 0.0)
        inner = inner * jnp.dot(x, wu[...], preferred_element_type=F32)
        out = jnp.dot(inner.astype(BF16), wd[...], preferred_element_type=F32)
        partial[owner] = (out * gate).astype(BF16)

    def return_copy(half, subset, arriving):
        k = subset.bit_length() - 1
        start, size = spans[half]
        owner = flip(me, flips_of(half, subset))
        sem = half * n_ex + subset
        return pltpu.make_async_remote_copy(
            src_ref=partial.at[owner, pl.ds(start, size)], dst_ref=inbox.at[subset, pl.ds(start, size)],
            send_sem=r_s.at[sem], recv_sem=r_r.at[sem],
            device_id={"expert": flip(me, [orders[half][k]])}, device_id_type=MESH)

    def collect(half, subset):
        return_copy(half, subset, True).wait_recv()
        k = subset.bit_length() - 1
        target = subset - (1 << k)
        if target:
            start, size = spans[half]
            rows = pl.ds(start, size)
            owner = flip(me, flips_of(half, target))
            both = partial[owner, rows].astype(F32) + inbox[subset, rows].astype(F32)
            partial[owner, rows] = both.astype(BF16)

    core = bits[0]
    groups = [[b for b in bits[1:] if m * 2 & b] for m in range(n_ex // 2)]
    groups.sort(key=len)

    def ready(flips):
        for half in range(2):
            subset = place(half, flips)
            collect(half, subset + (1 << (steps - 1)))
            if subset.bit_length() == steps - 1:
                return_copy(half, subset, False).start()

    done = []
    for i, flips in enumerate(groups):
        for half in range(2):
            subset = place(half, flips)
            if subset:
                take(half, subset)
                forward(half, subset)
        for half in range(2):
            take(half, place(half, flips + [core]))
        far = flip(me, flips)

        def pair(j, carry):
            expert(far + j * (core - 2 * core * ((far // core) % 2)))
            return carry

        lax.fori_loop(0, 2, pair, 0)
        for half in range(2):
            return_copy(half, place(half, flips + [core]), False).start()
        if done:
            ready(done[-1])
        done.append(flips)
    ready(done[-1])
    for k in range(steps - 2, -1, -1):
        for half in range(2):
            for subset in range(1 << k, 2 << k):
                if k < steps - 2:
                    return_copy(half, subset, False).start()
        for half in range(2):
            for subset in range(1 << k, 2 << k):
                collect(half, subset)
    for half in range(2):
        start, size = spans[half]
        rows = pl.ds(start, size)
        total = partial[me, rows].astype(F32)
        for k in range(steps):
            total += inbox[1 << k, rows].astype(F32)
        keep = min(size, count - start)
        layer_out[start:start + keep, :] = (hidden[start:start + keep, :] + total[0:keep]).astype(BF16)

    for d in range(1, n_dp):
        from_row(dep_k.at[0], got_k, mk_s, mk_r, d).wait_recv()
        from_row(dep_v.at[0], got_v, mv_s, mv_r, d).wait_recv()
    fresh_line = iota((context, 1), 0) == last_len
    for got, fresh, moved in ((got_k, fresh_k, moved_k), (got_v, fresh_v, moved_v)):
        new = fresh[0:16, :].astype(F32)[DEC - 1:DEC, :]
        picked = jnp.zeros(got.shape[1:], F32)
        for i in range(n_dp):
            picked = jnp.where(destination[0, i] == row, got[i].astype(F32), picked)
        moved[0] = jnp.where(fresh_line, new, picked).astype(BF16)

    for d in range(1, n_dp):
        to_row(ask, asked, ask_s, ask_r, d).wait_send()
        reply(d, row).wait_send()
        to_row(dep_k.at[0], got_k, mk_s, mk_r, d).wait_send()
        to_row(dep_v.at[0], got_v, mv_s, mv_r, d).wait_send()
    for d in range(1, n_ex):
        mask_copy(d, me).wait_send()
    for half in range(2):
        for k in range(steps):
            for subset in range(1 << k):
                gather_copy(half, subset, k, False).wait_send()
        for subset in range(1, n_ex):
            return_copy(half, subset, False).wait_send()


def on_device(
    n_dp, n_ex,
    queries, fresh_keys, fresh_values, residual, norm_gain, out_weight, router_weight,
    gate_weight, up_weight, down_weight, expert_ids, paged_keys, paged_values,
    decode_table, prefill_table, decode_len, prefill_len, departing_keys, departing_values, destination,
):
    count, width = queries.shape
    padded = (count + 15) // 16 * 16
    hidden_units = gate_weight.shape[2]
    cache = departing_keys.shape[1:]
    vmem = pl.BlockSpec(memory_space=pltpu.VMEM)
    smem = pl.BlockSpec(memory_space=pltpu.SMEM)
    anywhere = pl.BlockSpec(memory_space=pl.ANY)
    dma = pltpu.SemaphoreType.DMA
    return pl.pallas_call(
        functools.partial(kernel, n_dp, n_ex),
        out_shape=(
            jax.ShapeDtypeStruct((count, width), BF16),
            jax.ShapeDtypeStruct(departing_keys.shape, BF16),
            jax.ShapeDtypeStruct(departing_values.shape, BF16),
        ),
        in_specs=[smem] * 5 + [vmem] * 11 + [anywhere] * 4,
        out_specs=(vmem, vmem, vmem),
        scratch_shapes=[
            pltpu.VMEM((width, width), BF16),
            pltpu.VMEM((width, hidden_units), BF16),
            pltpu.VMEM((width, hidden_units), BF16),
            pltpu.VMEM((hidden_units, width), BF16),
            pltpu.VMEM((count, width), F32),
            pltpu.VMEM((count, width), F32),
            pltpu.VMEM((n_ex, padded, HEAD), BF16),
            pltpu.VMEM((n_ex, padded, width), BF16),
            pltpu.VMEM((n_ex, padded, width), BF16),
            pltpu.VMEM((n_ex, padded, width), BF16),
            pltpu.VMEM((16, HEAD), BF16),
            pltpu.VMEM((n_dp, 32, HEAD), F32),
            pltpu.VMEM((n_dp, 16, HEAD), BF16),
            pltpu.VMEM((n_dp, 32, HEAD), F32),
            pltpu.VMEM((n_dp,) + cache, BF16),
            pltpu.VMEM((n_dp,) + cache, BF16),
            dma((4,)),
            dma((n_dp,)), dma((n_dp,)), dma((n_dp,)), dma((n_dp,)),
            dma((n_dp,)), dma((n_dp,)), dma((n_dp,)), dma((n_dp,)),
            dma((n_ex,)), dma((n_ex,)),
            dma((2 * n_ex,)), dma((2 * n_ex,)), dma((2 * n_ex,)), dma((2 * n_ex,)),
        ],
        compiler_params=pltpu.CompilerParams(
            collective_id=0, has_side_effects=True, vmem_limit_bytes=56 * 1024 * 1024
        ),
    )(
        decode_table, prefill_table, decode_len, prefill_len, destination,
        queries, fresh_keys, fresh_values, residual, norm_gain.reshape(1, width), router_weight,
        expert_ids, paged_keys, paged_values, departing_keys, departing_values,
        out_weight, gate_weight, up_weight, down_weight,
    )


def solution(mesh):
    both = ("dp", "expert")
    return jax.shard_map(
        functools.partial(on_device, mesh.shape["dp"], mesh.shape["expert"]),
        mesh=mesh,
        in_specs=(
            P(both, None), P(both, None), P(both, None), P(both, None),
            P(), P(), P(),
            P("expert", None, None), P("expert", None, None), P("expert", None, None),
            P(both, None),
            P(both, None, None), P(both, None, None),
            P(both, None), P(both, None), P(both, None), P(both),
            P(both, None, None), P(both, None, None),
            P("expert", None),
        ),
        out_specs=(P(both, None), P(both, None, None), P(both, None, None)),
        check_vma=False,
    )
```

```python
import functools

import jax
import jax.numpy as jnp
from jax import lax
from jax.experimental import pallas as pl
from jax.experimental.pallas import tpu as pltpu
from jax.sharding import PartitionSpec as P

QUERY_HEADS = 12
KEY_VALUE_HEADS = 2
GROUP = QUERY_HEADS // KEY_VALUE_HEADS
HEAD = 128
DEC = 8
SCALE = HEAD ** (-0.5)
MESH = pl.DeviceIdType.MESH
F32 = jnp.float32
BF16 = jnp.bfloat16
NT = (((1,), (1,)), ((), ()))


def iota(shape, dim):
    return lax.broadcasted_iota(jnp.int32, shape, dim)


def kernel(
    n_dp, n_ex,
    dec_table, pre_table, dec_len, pre_len, destination,
    queries, fresh_k, fresh_v, residual, gain, router, ids, pool_k, pool_v, dep_k, dep_v,
    out_w, gate_w, up_w, down_w,
    layer_out, moved_k, moved_v,
    wo, wg, wu, wd, hidden, attended, masks, tokens, partial, inbox,
    ask, answer, asked, answered, far_kv, near_out, near_in,
    w_sem, ask_s, ask_r, ans_s, ans_r, far_s, far_r, near_s, near_r, msk_s, msk_r, g_s, g_r, r_s, r_r,
):
    row = lax.axis_index("dp")
    me = lax.axis_index("expert")
    count = queries.shape[0]
    padded = tokens.shape[1]
    cut = (padded // 2 + 15) // 16 * 16
    spans = ((0, cut), (cut, padded - cut))
    pool_pages, page = pool_k.shape[0], pool_k.shape[1]
    context = dep_k.shape[1]
    steps = n_ex.bit_length() - 1
    bits = [1 << b for b in range(steps)]
    orders = (bits[1:] + bits[:1], bits[1:][::-1] + bits[:1])

    weights = [
        pltpu.make_async_copy(src, dst, w_sem.at[i])
        for i, (src, dst) in enumerate(((out_w, wo), (gate_w.at[0], wg), (up_w.at[0], wu), (down_w.at[0], wd)))
    ]
    for copy in weights:
        copy.start()

    barrier = pltpu.get_barrier_semaphore()
    for d in range(1, n_dp):
        pl.semaphore_signal(barrier, inc=1, device_id={"dp": (row + d) % n_dp}, device_id_type=MESH)
    for d in range(1, n_ex):
        pl.semaphore_signal(barrier, inc=1, device_id={"expert": (me + d) % n_ex}, device_id_type=MESH)
    pl.semaphore_wait(barrier, n_dp + n_ex - 2)

    last = queries[0:16, :].astype(F32)[DEC - 1:DEC, :]
    line = iota((16, HEAD), 0)
    message = jnp.zeros((16, HEAD), F32)
    for h in range(QUERY_HEADS):
        message = jnp.where(line == h, last[:, h * HEAD:(h + 1) * HEAD], message)
    last_len = dec_len[0, DEC - 1]
    message = jnp.where(line == QUERY_HEADS, (last_len // 16).astype(F32), message)
    message = jnp.where(line == QUERY_HEADS + 1, (last_len % 16).astype(F32), message)
    ask[...] = message.astype(BF16)
    asked[row] = message.astype(BF16)

    def to_row(src, dst, send, recv, d):
        return pltpu.make_async_remote_copy(
            src_ref=src, dst_ref=dst.at[row], send_sem=send.at[d], recv_sem=recv.at[d],
            device_id={"dp": (row + d) % n_dp}, device_id_type=MESH)

    def from_row(src, dst, send, recv, d):
        return pltpu.make_async_remote_copy(
            src_ref=src, dst_ref=dst.at[(row + n_dp - d) % n_dp], send_sem=send.at[d], recv_sem=recv.at[d],
            device_id={"dp": (row + d) % n_dp}, device_id_type=MESH)

    for d in range(1, n_dp):
        to_row(ask, asked, ask_s, ask_r, d).start()

    chose = jnp.zeros((HEAD, count), F32)
    line = iota((HEAD, count), 0)
    for k in range(ids.shape[0]):
        chose = jnp.where(ids[k:k + 1, :] == line, 1.0, chose)
    chose = jnp.transpose(chose)
    masks[me] = jnp.concatenate([chose, jnp.zeros((padded - count, HEAD), F32)], axis=0).astype(BF16)

    def mask_copy(d, slot):
        return pltpu.make_async_remote_copy(
            src_ref=masks.at[slot], dst_ref=masks.at[slot], send_sem=msk_s.at[d], recv_sem=msk_r.at[d],
            device_id={"expert": (me + d) % n_ex}, device_id_type=MESH)

    for d in range(1, n_ex):
        mask_copy(d, me).start()

    small = iota((16, page), 0)
    spot = iota((16, page), 1)
    lens = jnp.zeros((16, page), jnp.int32)
    tables = [jnp.full((16, page), -1, jnp.int32) for _ in range(dec_table.shape[0])]
    for s in range(DEC - 1):
        lens = jnp.where(small == s, dec_len[0, s], lens)
        for p in range(len(tables)):
            tables[p] = jnp.where(small == s, dec_table[p, s], tables[p])
    pieces = []
    for g in range(pool_pages):
        piece = jnp.zeros((16, page), F32)
        for p, table in enumerate(tables):
            piece += jnp.where((table == g) & (spot + p * page < lens), 1.0, 0.0)
        pieces.append(piece)
    times = jnp.concatenate(pieces, axis=1)
    times = jnp.concatenate([times] * GROUP, axis=0)

    def decode_part(kh):
        cols = slice(kh * HEAD, (kh + 1) * HEAD)
        q = jnp.concatenate(
            [queries[0:16, (kh * GROUP + g) * HEAD:(kh * GROUP + g + 1) * HEAD] for g in range(GROUP)], axis=0)
        keys = pool_k[:, :, cols].reshape(pool_pages * page, HEAD)
        values = pool_v[:, :, cols].reshape(pool_pages * page, HEAD)
        s = lax.dot_general(q, keys, NT, preferred_element_type=F32) * SCALE
        w = jnp.exp(s) * times
        return jnp.dot(w.astype(BF16), values, preferred_element_type=F32), jnp.sum(w, axis=1, keepdims=True)

    decoded = [decode_part(kh) for kh in range(KEY_VALUE_HEADS)]

    for d in range(1, n_dp):
        from_row(ask, asked, ask_s, ask_r, d).wait_recv()
    q = asked[...].reshape(n_dp * 16, HEAD)
    meta = asked[...].astype(F32)
    limits = meta[:, QUERY_HEADS:QUERY_HEADS + 1, 0:1] * 16.0 + meta[:, QUERY_HEADS + 1:QUERY_HEADS + 2, 0:1]
    limits = jnp.broadcast_to(limits, (n_dp, 16, 1)).reshape(n_dp * 16, 1)
    live = iota((n_dp * 16, context), 1).astype(F32) < limits
    head_line = iota((n_dp * 16, 1), 0) % 16
    sums, totals = None, None
    for kh in range(KEY_VALUE_HEADS):
        cols = slice(kh * HEAD, (kh + 1) * HEAD)
        s = lax.dot_general(q, dep_k[0, :, cols], NT, preferred_element_type=F32) * SCALE
        mine = (head_line >= kh * GROUP) & (head_line < (kh + 1) * GROUP)
        w = jnp.where(live & mine, jnp.exp(s), 0.0)
        mixed = jnp.dot(w.astype(BF16), dep_v[0, :, cols], preferred_element_type=F32)
        total = jnp.sum(w, axis=1, keepdims=True)
        sums = mixed if sums is None else sums + mixed
        totals = total if totals is None else totals + total
    answer[:, 0:16, :] = sums.reshape(n_dp, 16, HEAD)
    answer[:, 16:32, :] = jnp.broadcast_to(totals, (n_dp * 16, HEAD)).reshape(n_dp, 16, HEAD)
    answered[row] = answer[row]

    def reply(d, slot):
        return pltpu.make_async_remote_copy(
            src_ref=answer.at[(row + d) % n_dp], dst_ref=answered.at[slot],
            send_sem=ans_s.at[d], recv_sem=ans_r.at[d],
            device_id={"dp": (row + d) % n_dp}, device_id_type=MESH)

    for d in range(1, n_dp):
        reply(d, row).start()

    r = iota((count, context), 0)
    c = iota((count, context), 1)
    context_valid = (r >= DEC) & (c < pre_len[0])
    r = iota((count, count), 0)
    c = iota((count, count), 1)
    fresh_valid = (c <= r) & ((c >= DEC) | (c == r))
    fresh_parts = []
    for kh in range(KEY_VALUE_HEADS):
        cols = slice(kh * HEAD, (kh + 1) * HEAD)
        picks = [pre_table[0, p] for p in range(pre_table.shape[1])]
        keys = jnp.concatenate([pool_k[p, :, cols] for p in picks], axis=0)
        values = jnp.concatenate([pool_v[p, :, cols] for p in picks], axis=0)
        for g in range(GROUP):
            h = kh * GROUP + g
            q = queries[:, h * HEAD:(h + 1) * HEAD]
            s = lax.dot_general(q, keys, NT, preferred_element_type=F32) * SCALE
            w = jnp.where(context_valid, jnp.exp(s), 0.0)
            s = lax.dot_general(q, fresh_k[:, cols], NT, preferred_element_type=F32) * SCALE
            wf = jnp.where(fresh_valid, jnp.exp(s), 0.0)
            total = jnp.sum(w, axis=1, keepdims=True) + jnp.sum(wf, axis=1, keepdims=True)
            mixed = jnp.dot(w.astype(BF16), values, preferred_element_type=F32)
            mixed += jnp.dot(wf.astype(BF16), fresh_v[:, cols], preferred_element_type=F32)
            part, part_total = decoded[kh]
            fresh_parts.append((
                mixed[0:DEC] + part[g * 16:g * 16 + DEC],
                total[0:DEC] + part_total[g * 16:g * 16 + DEC],
            ))
            attended[DEC:count, h * HEAD:(h + 1) * HEAD] = mixed[DEC:] / total[DEC:]

    for d in range(1, n_dp):
        reply(d, (row + n_dp - d) % n_dp).wait_recv()
    arrived = jnp.zeros((32, HEAD), F32)
    for i in range(n_dp):
        arrived = jnp.where(destination[0, i] == row, answered[i], arrived)
    seventh = iota((DEC, HEAD), 0) == DEC - 1
    for h in range(QUERY_HEADS):
        mixed, total = fresh_parts[h]
        mixed = mixed + jnp.where(seventh, arrived[h:h + 1, :], 0.0)
        total = total + jnp.where(seventh, arrived[16 + h:17 + h, :], 0.0)
        attended[0:DEC, h * HEAD:(h + 1) * HEAD] = mixed / total

    weights[0].wait()
    x = residual[...].astype(F32) + jnp.dot(attended[...].astype(BF16), wo[...], preferred_element_type=F32)
    hidden[...] = x
    variance = jnp.mean(x * x, axis=-1, keepdims=True)
    normed = x * lax.rsqrt(variance + 1e-06) * gain[...][None, :]
    tokens[me] = jnp.concatenate([normed, jnp.zeros((padded - count, x.shape[1]), F32)], axis=0).astype(BF16)

    def flip(index, flips):
        for b in flips:
            index = index + b - 2 * b * ((index // b) % 2)
        return index

    def place(half, flips):
        return sum(1 << orders[half].index(b) for b in flips)

    def flips_of(half, subset):
        return [orders[half][k] for k in range(steps) if subset >> k & 1]

    def gather_copy(half, subset, k, arriving):
        start, size = spans[half]
        owner = flip(me, flips_of(half, subset + (1 << k) if arriving else subset))
        block = tokens.at[owner, pl.ds(start, size)]
        sem = half * n_ex + (1 << k) + subset
        return pltpu.make_async_remote_copy(
            src_ref=block, dst_ref=block, send_sem=g_s.at[sem], recv_sem=g_r.at[sem],
            device_id={"expert": flip(me, [orders[half][k]])}, device_id_type=MESH)

    def forward(half, subset):
        for k in range(subset.bit_length(), steps):
            gather_copy(half, subset, k, False).start()

    def take(half, subset):
        k = subset.bit_length() - 1
        gather_copy(half, subset - (1 << k), k, True).wait_recv()

    for half in range(2):
        forward(half, 0)

    halves = n_dp // 2
    across = (row + halves) % n_dp
    base, spot = row // halves * halves, row % halves
    leaving = (dep_k, dep_v)

    def far_copy(t):
        return pltpu.make_async_remote_copy(
            src_ref=leaving[t].at[0], dst_ref=far_kv.at[t], send_sem=far_s.at[t], recv_sem=far_r.at[t],
            device_id={"dp": across}, device_id_type=MESH)

    def near_copy(t, d, slot):
        sem = t * halves + d
        return pltpu.make_async_remote_copy(
            src_ref=near_out.at[t, d], dst_ref=near_in.at[t, slot], send_sem=near_s.at[sem],
            recv_sem=near_r.at[sem], device_id={"dp": base + (spot + d) % halves}, device_id_type=MESH)

    def choose(t, target, other):
        item = jnp.where(destination[0, across] == target, far_kv[t].astype(F32), other)
        return jnp.where(destination[0, row] == target, leaving[t][0].astype(F32), item)

    def hand_over(t):
        far_copy(t).wait_recv()
        for d in range(1, halves):
            target = base + (spot + d) % halves
            near_out[t, d] = choose(t, target, jnp.zeros((context, dep_k.shape[2]), F32)).astype(BF16)
            near_copy(t, d, spot).start()

    for t in range(2):
        far_copy(t).start()
    for d in range(1, n_ex):
        mask_copy(d, (me + n_ex - d) % n_ex).wait_recv()
    for copy in weights[1:]:
        copy.wait()

    def expert(owner):
        x = tokens[owner]
        logits = lax.dot_general(x, router[...], NT, preferred_element_type=F32)
        score = jax.nn.sigmoid(logits) * masks[owner].astype(F32)[:, 0:n_ex]
        total = jnp.sum(score, axis=1, keepdims=True)
        mine = jnp.sum(jnp.where(iota((padded, n_ex), 1) == me, score, 0.0), axis=1, keepdims=True)
        gate = mine / jnp.where(total == 0.0, 1.0, total)
        inner = jnp.maximum(jnp.dot(x, wg[...], preferred_element_type=F32), 0.0)
        inner = inner * jnp.dot(x, wu[...], preferred_element_type=F32)
        out = jnp.dot(inner.astype(BF16), wd[...], preferred_element_type=F32)
        partial[owner] = (out * gate).astype(BF16)

    def return_copy(half, subset, arriving):
        k = subset.bit_length() - 1
        start, size = spans[half]
        owner = flip(me, flips_of(half, subset))
        sem = half * n_ex + subset
        return pltpu.make_async_remote_copy(
            src_ref=partial.at[owner, pl.ds(start, size)], dst_ref=inbox.at[subset, pl.ds(start, size)],
            send_sem=r_s.at[sem], recv_sem=r_r.at[sem],
            device_id={"expert": flip(me, [orders[half][k]])}, device_id_type=MESH)

    def collect(half, subset):
        return_copy(half, subset, True).wait_recv()
        k = subset.bit_length() - 1
        target = subset - (1 << k)
        if target:
            start, size = spans[half]
            rows = pl.ds(start, size)
            owner = flip(me, flips_of(half, target))
            both = partial[owner, rows].astype(F32) + inbox[subset, rows].astype(F32)
            partial[owner, rows] = both.astype(BF16)

    core = bits[0]
    groups = [[b for b in bits[1:] if m * 2 & b] for m in range(n_ex // 2)]
    groups.sort(key=len)

    def ready(flips):
        for half in range(2):
            subset = place(half, flips)
            collect(half, subset + (1 << (steps - 1)))
            if subset.bit_length() == steps - 1:
                return_copy(half, subset, False).start()

    done = []
    for i, flips in enumerate(groups):
        for half in range(2):
            subset = place(half, flips)
            if subset:
                take(half, subset)
                forward(half, subset)
        for half in range(2):
            take(half, place(half, flips + [core]))
        far = flip(me, flips)

        def pair(j, carry):
            expert(far + j * (core - 2 * core * ((far // core) % 2)))
            return carry

        lax.fori_loop(0, 2, pair, 0)
        for half in range(2):
            return_copy(half, place(half, flips + [core]), False).start()
        if done:
            ready(done[-1])
        done.append(flips)
        if i == len(groups) - 2:
            hand_over(0)
    ready(done[-1])
    hand_over(1)
    for k in range(steps - 2, -1, -1):
        for half in range(2):
            for subset in range(1 << k, 2 << k):
                if k < steps - 2:
                    return_copy(half, subset, False).start()
        for half in range(2):
            for subset in range(1 << k, 2 << k):
                collect(half, subset)
    for half in range(2):
        start, size = spans[half]
        rows = pl.ds(start, size)
        total = partial[me, rows].astype(F32)
        for k in range(steps):
            total += inbox[1 << k, rows].astype(F32)
        keep = min(size, count - start)
        layer_out[start:start + keep, :] = (hidden[start:start + keep, :] + total[0:keep]).astype(BF16)

    fresh_line = iota((context, 1), 0) == last_len
    for t, (fresh, moved) in enumerate(((fresh_k, moved_k), (fresh_v, moved_v))):
        new = fresh[0:16, :].astype(F32)[DEC - 1:DEC, :]
        picked = jnp.zeros((context, dep_k.shape[2]), F32)
        for d in range(1, halves):
            slot = (spot + halves - d) % halves
            near_copy(t, d, slot).wait_recv()
            source = base + slot
            due = (destination[0, source] == row) | (destination[0, (source + halves) % n_dp] == row)
            picked = jnp.where(due, near_in[t, slot].astype(F32), picked)
        picked = choose(t, row, picked)
        moved[0] = jnp.where(fresh_line, new, picked).astype(BF16)

    for d in range(1, n_dp):
        to_row(ask, asked, ask_s, ask_r, d).wait_send()
        reply(d, row).wait_send()
    for t in range(2):
        far_copy(t).wait_send()
        for d in range(1, halves):
            near_copy(t, d, spot).wait_send()
    for d in range(1, n_ex):
        mask_copy(d, me).wait_send()
    for half in range(2):
        for k in range(steps):
            for subset in range(1 << k):
                gather_copy(half, subset, k, False).wait_send()
        for subset in range(1, n_ex):
            return_copy(half, subset, False).wait_send()


def write_out(*refs):
    for src, dst in zip(refs[:3], refs[3:]):
        dst[...] = src[...]


def on_device(
    n_dp, n_ex,
    queries, fresh_keys, fresh_values, residual, norm_gain, out_weight, router_weight,
    gate_weight, up_weight, down_weight, expert_ids, paged_keys, paged_values,
    decode_table, prefill_table, decode_len, prefill_len, departing_keys, departing_values, destination,
):
    count, width = queries.shape
    padded = (count + 15) // 16 * 16
    hidden_units = gate_weight.shape[2]
    cache = departing_keys.shape[1:]
    vmem = pl.BlockSpec(memory_space=pltpu.VMEM)
    smem = pl.BlockSpec(memory_space=pltpu.SMEM)
    anywhere = pl.BlockSpec(memory_space=pl.ANY)
    dma = pltpu.SemaphoreType.DMA
    results = pl.pallas_call(
        functools.partial(kernel, n_dp, n_ex),
        out_shape=(
            jax.ShapeDtypeStruct((count, width), BF16),
            jax.ShapeDtypeStruct(departing_keys.shape, BF16),
            jax.ShapeDtypeStruct(departing_values.shape, BF16),
        ),
        in_specs=[smem] * 5 + [vmem] * 11 + [anywhere] * 4,
        out_specs=(vmem, vmem, vmem),
        scratch_shapes=[
            pltpu.VMEM((width, width), BF16),
            pltpu.VMEM((width, hidden_units), BF16),
            pltpu.VMEM((width, hidden_units), BF16),
            pltpu.VMEM((hidden_units, width), BF16),
            pltpu.VMEM((count, width), F32),
            pltpu.VMEM((count, width), F32),
            pltpu.VMEM((n_ex, padded, HEAD), BF16),
            pltpu.VMEM((n_ex, padded, width), BF16),
            pltpu.VMEM((n_ex, padded, width), BF16),
            pltpu.VMEM((n_ex, padded, width), BF16),
            pltpu.VMEM((16, HEAD), BF16),
            pltpu.VMEM((n_dp, 32, HEAD), F32),
            pltpu.VMEM((n_dp, 16, HEAD), BF16),
            pltpu.VMEM((n_dp, 32, HEAD), F32),
            pltpu.VMEM((2,) + cache, BF16),
            pltpu.VMEM((2, n_dp // 2) + cache, BF16),
            pltpu.VMEM((2, n_dp // 2) + cache, BF16),
            dma((4,)),
            dma((n_dp,)), dma((n_dp,)), dma((n_dp,)), dma((n_dp,)),
            dma((2,)), dma((2,)), dma((n_dp,)), dma((n_dp,)),
            dma((n_ex,)), dma((n_ex,)),
            dma((2 * n_ex,)), dma((2 * n_ex,)), dma((2 * n_ex,)), dma((2 * n_ex,)),
        ],
        compiler_params=pltpu.CompilerParams(
            collective_id=0, has_side_effects=True, vmem_limit_bytes=56 * 1024 * 1024
        ),
    )(
        decode_table.T, prefill_table, decode_len, prefill_len, destination,
        queries, fresh_keys, fresh_values, residual, norm_gain, router_weight.T,
        expert_ids.T, paged_keys, paged_values, departing_keys, departing_values,
        out_weight, gate_weight, up_weight, down_weight,
    )
    return pl.pallas_call(
        write_out,
        out_shape=tuple(jax.ShapeDtypeStruct(x.shape, x.dtype) for x in results),
        in_specs=[vmem] * 3,
        out_specs=(vmem,) * 3,
    )(*results)


def solution(mesh):
    both = ("dp", "expert")
    return jax.shard_map(
        functools.partial(on_device, mesh.shape["dp"], mesh.shape["expert"]),
        mesh=mesh,
        in_specs=(
            P(both, None), P(both, None), P(both, None), P(both, None),
            P(), P(), P(),
            P("expert", None, None), P("expert", None, None), P("expert", None, None),
            P(both, None),
            P(both, None, None), P(both, None, None),
            P(both, None), P(both, None), P(both, None), P(both),
            P(both, None, None), P(both, None, None),
            P("expert", None),
        ),
        out_specs=(P(both, None), P(both, None, None), P(both, None, None)),
        check_vma=False,
    )
```

```python
import functools

import jax
import jax.numpy as jnp
from jax import lax
from jax.experimental import pallas as pl
from jax.experimental.pallas import tpu as pltpu
from jax.sharding import PartitionSpec as P

QUERY_HEADS = 12
KEY_VALUE_HEADS = 2
GROUP = QUERY_HEADS // KEY_VALUE_HEADS
HEAD = 128
DEC = 8
SCALE = HEAD ** (-0.5)
MESH = pl.DeviceIdType.MESH
F32 = jnp.float32
BF16 = jnp.bfloat16
NT = (((1,), (1,)), ((), ()))


def iota(shape, dim):
    return lax.broadcasted_iota(jnp.int32, shape, dim)


def kernel(
    n_dp, n_ex,
    dec_table, pre_table, dec_len, pre_len, destination,
    queries, fresh_k, fresh_v, residual, gain, router, ids, pool_k, pool_v, dep_k, dep_v,
    out_w, gate_w, up_w, down_w,
    layer_out, moved_k, moved_v,
    wo, wg, wu, wd, hidden, attended, masks, tokens, partial, inbox,
    ask, answer, asked, answered, far_kv, near_out, near_in,
    w_sem, ask_s, ask_r, ans_s, ans_r, far_s, far_r, near_s, near_r, msk_s, msk_r, g_s, g_r, r_s, r_r,
):
    row = lax.axis_index("dp")
    me = lax.axis_index("expert")
    count = queries.shape[0]
    padded = tokens.shape[1]
    cut = (padded // 2 + 15) // 16 * 16
    spans = ((0, cut), (cut, padded - cut))
    pool_pages, page = pool_k.shape[0], pool_k.shape[1]
    context = dep_k.shape[1]
    steps = n_ex.bit_length() - 1
    bits = [1 << b for b in range(steps)]
    orders = (bits[1:] + bits[:1], bits[1:][::-1] + bits[:1])

    weights = [
        pltpu.make_async_copy(src, dst, w_sem.at[i])
        for i, (src, dst) in enumerate(((out_w, wo), (gate_w.at[0], wg), (up_w.at[0], wu), (down_w.at[0], wd)))
    ]
    for copy in weights:
        copy.start()

    barrier = pltpu.get_barrier_semaphore()
    for d in range(1, n_dp):
        pl.semaphore_signal(barrier, inc=1, device_id={"dp": (row + d) % n_dp}, device_id_type=MESH)
    for d in range(1, n_ex):
        pl.semaphore_signal(barrier, inc=1, device_id={"expert": (me + d) % n_ex}, device_id_type=MESH)
    pl.semaphore_wait(barrier, n_dp + n_ex - 2)

    last = queries[0:16, :].astype(F32)[DEC - 1:DEC, :]
    line = iota((16, HEAD), 0)
    message = jnp.zeros((16, HEAD), F32)
    for h in range(QUERY_HEADS):
        message = jnp.where(line == h, last[:, h * HEAD:(h + 1) * HEAD], message)
    last_len = dec_len[0, DEC - 1]
    message = jnp.where(line == QUERY_HEADS, (last_len // 16).astype(F32), message)
    message = jnp.where(line == QUERY_HEADS + 1, (last_len % 16).astype(F32), message)
    ask[...] = message.astype(BF16)
    asked[row] = message.astype(BF16)

    def to_row(src, dst, send, recv, d):
        return pltpu.make_async_remote_copy(
            src_ref=src, dst_ref=dst.at[row], send_sem=send.at[d], recv_sem=recv.at[d],
            device_id={"dp": (row + d) % n_dp}, device_id_type=MESH)

    def from_row(src, dst, send, recv, d):
        return pltpu.make_async_remote_copy(
            src_ref=src, dst_ref=dst.at[(row + n_dp - d) % n_dp], send_sem=send.at[d], recv_sem=recv.at[d],
            device_id={"dp": (row + d) % n_dp}, device_id_type=MESH)

    for d in range(1, n_dp):
        to_row(ask, asked, ask_s, ask_r, d).start()

    chose = jnp.zeros((HEAD, count), F32)
    line = iota((HEAD, count), 0)
    for k in range(ids.shape[0]):
        chose = jnp.where(ids[k:k + 1, :] == line, 1.0, chose)
    chose = jnp.transpose(chose)
    masks[me] = jnp.concatenate([chose, jnp.zeros((padded - count, HEAD), F32)], axis=0).astype(BF16)

    def mask_copy(d, slot):
        return pltpu.make_async_remote_copy(
            src_ref=masks.at[slot], dst_ref=masks.at[slot], send_sem=msk_s.at[d], recv_sem=msk_r.at[d],
            device_id={"expert": (me + d) % n_ex}, device_id_type=MESH)

    for d in range(1, n_ex):
        mask_copy(d, me).start()

    small = iota((16, page), 0)
    spot = iota((16, page), 1)
    lens = jnp.zeros((16, page), jnp.int32)
    tables = [jnp.full((16, page), -1, jnp.int32) for _ in range(dec_table.shape[0])]
    for s in range(DEC - 1):
        lens = jnp.where(small == s, dec_len[0, s], lens)
        for p in range(len(tables)):
            tables[p] = jnp.where(small == s, dec_table[p, s], tables[p])
    pieces = []
    for g in range(pool_pages):
        piece = jnp.zeros((16, page), F32)
        for p, table in enumerate(tables):
            piece += jnp.where((table == g) & (spot + p * page < lens), 1.0, 0.0)
        pieces.append(piece)
    times = jnp.concatenate(pieces, axis=1)
    times = jnp.concatenate([times] * GROUP, axis=0)

    def decode_part(kh):
        cols = slice(kh * HEAD, (kh + 1) * HEAD)
        q = jnp.concatenate(
            [queries[0:16, (kh * GROUP + g) * HEAD:(kh * GROUP + g + 1) * HEAD] for g in range(GROUP)], axis=0)
        keys = pool_k[:, :, cols].reshape(pool_pages * page, HEAD)
        values = pool_v[:, :, cols].reshape(pool_pages * page, HEAD)
        s = lax.dot_general(q, keys, NT, preferred_element_type=F32) * SCALE
        w = jnp.exp(s) * times
        return jnp.dot(w.astype(BF16), values, preferred_element_type=F32), jnp.sum(w, axis=1, keepdims=True)

    decoded = [decode_part(kh) for kh in range(KEY_VALUE_HEADS)]

    for d in range(1, n_dp):
        from_row(ask, asked, ask_s, ask_r, d).wait_recv()
    q = asked[...].reshape(n_dp * 16, HEAD)
    meta = asked[...].astype(F32)
    limits = meta[:, QUERY_HEADS:QUERY_HEADS + 1, 0:1] * 16.0 + meta[:, QUERY_HEADS + 1:QUERY_HEADS + 2, 0:1]
    limits = jnp.broadcast_to(limits, (n_dp, 16, 1)).reshape(n_dp * 16, 1)
    live = iota((n_dp * 16, context), 1).astype(F32) < limits
    head_line = iota((n_dp * 16, 1), 0) % 16
    sums, totals = None, None
    for kh in range(KEY_VALUE_HEADS):
        cols = slice(kh * HEAD, (kh + 1) * HEAD)
        s = lax.dot_general(q, dep_k[0, :, cols], NT, preferred_element_type=F32) * SCALE
        mine = (head_line >= kh * GROUP) & (head_line < (kh + 1) * GROUP)
        w = jnp.where(live & mine, jnp.exp(s), 0.0)
        mixed = jnp.dot(w.astype(BF16), dep_v[0, :, cols], preferred_element_type=F32)
        total = jnp.sum(w, axis=1, keepdims=True)
        sums = mixed if sums is None else sums + mixed
        totals = total if totals is None else totals + total
    answer[:, 0:16, :] = sums.reshape(n_dp, 16, HEAD)
    answer[:, 16:32, :] = jnp.broadcast_to(totals, (n_dp * 16, HEAD)).reshape(n_dp, 16, HEAD)
    answered[row] = answer[row]

    def reply(d, slot):
        return pltpu.make_async_remote_copy(
            src_ref=answer.at[(row + d) % n_dp], dst_ref=answered.at[slot],
            send_sem=ans_s.at[d], recv_sem=ans_r.at[d],
            device_id={"dp": (row + d) % n_dp}, device_id_type=MESH)

    for d in range(1, n_dp):
        reply(d, row).start()

    r = iota((count, context), 0)
    c = iota((count, context), 1)
    context_valid = (r >= DEC) & (c < pre_len[0])
    r = iota((count, count), 0)
    c = iota((count, count), 1)
    fresh_valid = (c <= r) & ((c >= DEC) | (c == r))
    fresh_parts = []
    for kh in range(KEY_VALUE_HEADS):
        cols = slice(kh * HEAD, (kh + 1) * HEAD)
        picks = [pre_table[0, p] for p in range(pre_table.shape[1])]
        keys = jnp.concatenate([pool_k[p, :, cols] for p in picks], axis=0)
        values = jnp.concatenate([pool_v[p, :, cols] for p in picks], axis=0)
        for g in range(GROUP):
            h = kh * GROUP + g
            q = queries[:, h * HEAD:(h + 1) * HEAD]
            s = lax.dot_general(q, keys, NT, preferred_element_type=F32) * SCALE
            w = jnp.where(context_valid, jnp.exp(s), 0.0)
            s = lax.dot_general(q, fresh_k[:, cols], NT, preferred_element_type=F32) * SCALE
            wf = jnp.where(fresh_valid, jnp.exp(s), 0.0)
            total = jnp.sum(w, axis=1, keepdims=True) + jnp.sum(wf, axis=1, keepdims=True)
            mixed = jnp.dot(w.astype(BF16), values, preferred_element_type=F32)
            mixed += jnp.dot(wf.astype(BF16), fresh_v[:, cols], preferred_element_type=F32)
            part, part_total = decoded[kh]
            fresh_parts.append((
                mixed[0:DEC] + part[g * 16:g * 16 + DEC],
                total[0:DEC] + part_total[g * 16:g * 16 + DEC],
            ))
            attended[DEC:count, h * HEAD:(h + 1) * HEAD] = mixed[DEC:] / total[DEC:]

    for d in range(1, n_dp):
        reply(d, (row + n_dp - d) % n_dp).wait_recv()

    halves = n_dp // 2
    across = (row + halves) % n_dp
    base, spot = row // halves * halves, row % halves
    leaving = (dep_k, dep_v)

    def far_copy(t):
        return pltpu.make_async_remote_copy(
            src_ref=leaving[t].at[0], dst_ref=far_kv.at[t], send_sem=far_s.at[t], recv_sem=far_r.at[t],
            device_id={"dp": across}, device_id_type=MESH)

    def near_copy(t, d, slot):
        sem = t * halves + d
        return pltpu.make_async_remote_copy(
            src_ref=near_out.at[t, d], dst_ref=near_in.at[t, slot], send_sem=near_s.at[sem],
            recv_sem=near_r.at[sem], device_id={"dp": base + (spot + d) % halves}, device_id_type=MESH)

    def choose(t, target, other):
        item = jnp.where(destination[0, across] == target, far_kv[t].astype(F32), other)
        return jnp.where(destination[0, row] == target, leaving[t][0].astype(F32), item)

    def hand_over(t):
        far_copy(t).wait_recv()
        for d in range(1, halves):
            target = base + (spot + d) % halves
            near_out[t, d] = choose(t, target, jnp.zeros((context, dep_k.shape[2]), F32)).astype(BF16)
            near_copy(t, d, spot).start()

    for t in range(2):
        far_copy(t).start()
    arrived = jnp.zeros((32, HEAD), F32)
    for i in range(n_dp):
        arrived = jnp.where(destination[0, i] == row, answered[i], arrived)
    seventh = iota((DEC, HEAD), 0) == DEC - 1
    for h in range(QUERY_HEADS):
        mixed, total = fresh_parts[h]
        mixed = mixed + jnp.where(seventh, arrived[h:h + 1, :], 0.0)
        total = total + jnp.where(seventh, arrived[16 + h:17 + h, :], 0.0)
        attended[0:DEC, h * HEAD:(h + 1) * HEAD] = mixed / total

    weights[0].wait()
    x = residual[...].astype(F32) + jnp.dot(attended[...].astype(BF16), wo[...], preferred_element_type=F32)
    hidden[...] = x
    variance = jnp.mean(x * x, axis=-1, keepdims=True)
    normed = x * lax.rsqrt(variance + 1e-06) * gain[...][None, :]
    tokens[me] = jnp.concatenate([normed, jnp.zeros((padded - count, x.shape[1]), F32)], axis=0).astype(BF16)

    def flip(index, flips):
        for b in flips:
            index = index + b - 2 * b * ((index // b) % 2)
        return index

    def place(half, flips):
        return sum(1 << orders[half].index(b) for b in flips)

    def flips_of(half, subset):
        return [orders[half][k] for k in range(steps) if subset >> k & 1]

    def gather_copy(half, subset, k, arriving):
        start, size = spans[half]
        owner = flip(me, flips_of(half, subset + (1 << k) if arriving else subset))
        block = tokens.at[owner, pl.ds(start, size)]
        sem = half * n_ex + (1 << k) + subset
        return pltpu.make_async_remote_copy(
            src_ref=block, dst_ref=block, send_sem=g_s.at[sem], recv_sem=g_r.at[sem],
            device_id={"expert": flip(me, [orders[half][k]])}, device_id_type=MESH)

    def forward(half, subset):
        for k in range(subset.bit_length(), steps):
            gather_copy(half, subset, k, False).start()

    def take(half, subset):
        k = subset.bit_length() - 1
        gather_copy(half, subset - (1 << k), k, True).wait_recv()

    for k in range(steps):
        for half in range(2):
            gather_copy(half, 0, k, False).start()

    for d in range(1, n_ex):
        mask_copy(d, (me + n_ex - d) % n_ex).wait_recv()
    for copy in weights[1:]:
        copy.wait()

    def expert(owner):
        x = tokens[owner]
        logits = lax.dot_general(x, router[...], NT, preferred_element_type=F32)
        score = jax.nn.sigmoid(logits) * masks[owner].astype(F32)[:, 0:n_ex]
        total = jnp.sum(score, axis=1, keepdims=True)
        mine = jnp.sum(jnp.where(iota((padded, n_ex), 1) == me, score, 0.0), axis=1, keepdims=True)
        gate = mine / jnp.where(total == 0.0, 1.0, total)
        inner = jnp.maximum(jnp.dot(x, wg[...], preferred_element_type=F32), 0.0)
        inner = inner * jnp.dot(x, wu[...], preferred_element_type=F32)
        out = jnp.dot(inner.astype(BF16), wd[...], preferred_element_type=F32)
        partial[owner] = (out * gate).astype(BF16)

    def return_copy(half, subset, arriving):
        k = subset.bit_length() - 1
        start, size = spans[half]
        owner = flip(me, flips_of(half, subset))
        sem = half * n_ex + subset
        return pltpu.make_async_remote_copy(
            src_ref=partial.at[owner, pl.ds(start, size)], dst_ref=inbox.at[subset, pl.ds(start, size)],
            send_sem=r_s.at[sem], recv_sem=r_r.at[sem],
            device_id={"expert": flip(me, [orders[half][k]])}, device_id_type=MESH)

    def collect(half, subset):
        return_copy(half, subset, True).wait_recv()
        k = subset.bit_length() - 1
        target = subset - (1 << k)
        if target:
            start, size = spans[half]
            rows = pl.ds(start, size)
            owner = flip(me, flips_of(half, target))
            both = partial[owner, rows].astype(F32) + inbox[subset, rows].astype(F32)
            partial[owner, rows] = both.astype(BF16)

    core = bits[0]
    groups = [[b for b in bits[1:] if m * 2 & b] for m in range(n_ex // 2)]
    groups.sort(key=len)

    def ready(flips):
        for half in range(2):
            subset = place(half, flips)
            collect(half, subset + (1 << (steps - 1)))
            if subset.bit_length() == steps - 1:
                return_copy(half, subset, False).start()

    done = []
    for i, flips in enumerate(groups):
        for half in range(2):
            subset = place(half, flips)
            if subset:
                take(half, subset)
                forward(half, subset)
        far = flip(me, flips)

        def pair(j, carry):
            @pl.when(j == 1)
            def _():
                for half in range(2):
                    take(half, place(half, flips + [core]))

            expert(far + j * (core - 2 * core * ((far // core) % 2)))
            return carry

        lax.fori_loop(0, 2, pair, 0)
        for half in range(2):
            return_copy(half, place(half, flips + [core]), False).start()
        if done:
            ready(done[-1])
        done.append(flips)
        if i == len(groups) - 2:
            hand_over(0)
    ready(done[-1])
    hand_over(1)
    for k in range(steps - 2, -1, -1):
        for half in range(2):
            for subset in range(1 << k, 2 << k):
                if k < steps - 2:
                    return_copy(half, subset, False).start()
        for half in range(2):
            for subset in range(1 << k, 2 << k):
                collect(half, subset)
    for half in range(2):
        start, size = spans[half]
        rows = pl.ds(start, size)
        total = partial[me, rows].astype(F32)
        for k in range(steps):
            total += inbox[1 << k, rows].astype(F32)
        keep = min(size, count - start)
        layer_out[start:start + keep, :] = (hidden[start:start + keep, :] + total[0:keep]).astype(BF16)

    fresh_line = iota((context, 1), 0) == last_len
    for t, (fresh, moved) in enumerate(((fresh_k, moved_k), (fresh_v, moved_v))):
        new = fresh[0:16, :].astype(F32)[DEC - 1:DEC, :]
        picked = jnp.zeros((context, dep_k.shape[2]), F32)
        for d in range(1, halves):
            slot = (spot + halves - d) % halves
            near_copy(t, d, slot).wait_recv()
            source = base + slot
            due = (destination[0, source] == row) | (destination[0, (source + halves) % n_dp] == row)
            picked = jnp.where(due, near_in[t, slot].astype(F32), picked)
        picked = choose(t, row, picked)
        moved[0] = jnp.where(fresh_line, new, picked).astype(BF16)

    for d in range(1, n_dp):
        to_row(ask, asked, ask_s, ask_r, d).wait_send()
        reply(d, row).wait_send()
    for t in range(2):
        far_copy(t).wait_send()
        for d in range(1, halves):
            near_copy(t, d, spot).wait_send()
    for d in range(1, n_ex):
        mask_copy(d, me).wait_send()
    for half in range(2):
        for k in range(steps):
            for subset in range(1 << k):
                gather_copy(half, subset, k, False).wait_send()
        for subset in range(1, n_ex):
            return_copy(half, subset, False).wait_send()


def write_out(*refs):
    for src, dst in zip(refs[:3], refs[3:]):
        dst[...] = src[...]


def on_device(
    n_dp, n_ex,
    queries, fresh_keys, fresh_values, residual, norm_gain, out_weight, router_weight,
    gate_weight, up_weight, down_weight, expert_ids, paged_keys, paged_values,
    decode_table, prefill_table, decode_len, prefill_len, departing_keys, departing_values, destination,
):
    count, width = queries.shape
    padded = (count + 15) // 16 * 16
    hidden_units = gate_weight.shape[2]
    cache = departing_keys.shape[1:]
    vmem = pl.BlockSpec(memory_space=pltpu.VMEM)
    smem = pl.BlockSpec(memory_space=pltpu.SMEM)
    anywhere = pl.BlockSpec(memory_space=pl.ANY)
    dma = pltpu.SemaphoreType.DMA
    results = pl.pallas_call(
        functools.partial(kernel, n_dp, n_ex),
        out_shape=(
            jax.ShapeDtypeStruct((count, width), BF16),
            jax.ShapeDtypeStruct(departing_keys.shape, BF16),
            jax.ShapeDtypeStruct(departing_values.shape, BF16),
        ),
        in_specs=[smem] * 5 + [vmem] * 11 + [anywhere] * 4,
        out_specs=(vmem, vmem, vmem),
        scratch_shapes=[
            pltpu.VMEM((width, width), BF16),
            pltpu.VMEM((width, hidden_units), BF16),
            pltpu.VMEM((width, hidden_units), BF16),
            pltpu.VMEM((hidden_units, width), BF16),
            pltpu.VMEM((count, width), F32),
            pltpu.VMEM((count, width), F32),
            pltpu.VMEM((n_ex, padded, HEAD), BF16),
            pltpu.VMEM((n_ex, padded, width), BF16),
            pltpu.VMEM((n_ex, padded, width), BF16),
            pltpu.VMEM((n_ex, padded, width), BF16),
            pltpu.VMEM((16, HEAD), BF16),
            pltpu.VMEM((n_dp, 32, HEAD), F32),
            pltpu.VMEM((n_dp, 16, HEAD), BF16),
            pltpu.VMEM((n_dp, 32, HEAD), F32),
            pltpu.VMEM((2,) + cache, BF16),
            pltpu.VMEM((2, n_dp // 2) + cache, BF16),
            pltpu.VMEM((2, n_dp // 2) + cache, BF16),
            dma((4,)),
            dma((n_dp,)), dma((n_dp,)), dma((n_dp,)), dma((n_dp,)),
            dma((2,)), dma((2,)), dma((n_dp,)), dma((n_dp,)),
            dma((n_ex,)), dma((n_ex,)),
            dma((2 * n_ex,)), dma((2 * n_ex,)), dma((2 * n_ex,)), dma((2 * n_ex,)),
        ],
        compiler_params=pltpu.CompilerParams(
            collective_id=0, has_side_effects=True, vmem_limit_bytes=56 * 1024 * 1024
        ),
    )(
        decode_table.T, prefill_table, decode_len, prefill_len, destination,
        queries, fresh_keys, fresh_values, residual, norm_gain, router_weight.T,
        expert_ids.T, paged_keys, paged_values, departing_keys, departing_values,
        out_weight, gate_weight, up_weight, down_weight,
    )
    return pl.pallas_call(
        write_out,
        out_shape=tuple(jax.ShapeDtypeStruct(x.shape, x.dtype) for x in results),
        in_specs=[vmem] * 3,
        out_specs=(vmem,) * 3,
    )(*results)


def solution(mesh):
    both = ("dp", "expert")
    return jax.shard_map(
        functools.partial(on_device, mesh.shape["dp"], mesh.shape["expert"]),
        mesh=mesh,
        in_specs=(
            P(both, None), P(both, None), P(both, None), P(both, None),
            P(), P(), P(),
            P("expert", None, None), P("expert", None, None), P("expert", None, None),
            P(both, None),
            P(both, None, None), P(both, None, None),
            P(both, None), P(both, None), P(both, None), P(both),
            P(both, None, None), P(both, None, None),
            P("expert", None),
        ),
        out_specs=(P(both, None), P(both, None, None), P(both, None, None)),
        check_vma=False,
    )
```
